32 devices in a mesh: node: 4 (over z), space: 8 (over y, x, core).
Axes of the slice: x: 2, y: 2, z: 4, core: 2. Of those that a mesh axis runs over, the one named last changes fastest.
Arguments:
- initial: float32 [2, 64, 16, 512], P(None, 'space'), may hold values from 0 to 1
- node_guess: float32 [8, 2, 64, 16, 512], P('node', None, 'space'), may hold values from 0 to 1
- region_codes: int32 [64, 16, 512], P('space'), may hold values from 0 to 7
- coeff_table: float32 [8, 2], replicated, may hold values from 0.25 to 2
Outputs:
- node_values: float32 [8, 2, 64, 16, 512], P('node', None, 'space')
The draws below stay inside these ranges and needn't reach their ends.
All inputs are finite; a program needn't handle non-finite values.
Results may differ from the reference program's by a relative error of at most 0.0001.
Values sent between devices are 32-bit elements; how exact they have to be, the bound alone decides.
A program may use at most 64 MiB of HBM per device.

```python
import math
import jax
import jax.numpy as jnp
import numpy as np
from jax import lax

NY = 512
NZ = 16
SWEEPS = 2
JACOBI = 6
REGIONS = 8
NODES = 8
NX = 64


def set_ends(array, stream_key, smallest, high):
    dims = array.shape
    place = [jax.random.randint(jax.random.fold_in(stream_key, axis), (), 0, dims[axis]) for axis in range(len(dims))]
    array = array.at[tuple(place)].set(smallest)
    longest = dims.index(max(dims))
    place[longest] = (place[longest] + 1) % dims[longest]
    return array.at[tuple(place)].set(high)


def level_of(own_key, shape, cuts, least, top_value):
    gain = 1.0
    for axis_at, parts in cuts:
        heights = jax.random.uniform(jax.random.fold_in(jax.random.fold_in(own_key, 6), axis_at), (parts,), jnp.float32, least / len(cuts), top_value / len(cuts))
        gain = gain * jnp.repeat(jnp.exp(heights), shape[axis_at] // parts).reshape((-1,) + (1,) * (len(shape) - 1 - axis_at))
    return gain


def setup_inputs(seed: int = 0) -> dict:
    key_list = jax.random.split(jax.random.key(seed), 5)
    return {
        "initial": jnp.clip(1.0 * jax.random.uniform(key_list[0], (2, NX, NZ, NY), jnp.float32) ** level_of(key_list[0], (2, NX, NZ, NY), ((1, 8),), -0.2, 0.2), 0.0, 1.0),
        "node_guess": jnp.clip(1.0 * jax.random.uniform(key_list[1], (NODES, 2, NX, NZ, NY), jnp.float32) ** level_of(key_list[1], (NODES, 2, NX, NZ, NY), ((0, 4), (2, 8)), -0.2, 0.2), 0.0, 1.0),
        "region_codes": set_ends(jax.random.randint(key_list[2], (NX, NZ, NY), 0, REGIONS), jax.random.fold_in(key_list[2], 1), 0, REGIONS - 1).astype(jnp.int32),
        "coeff_table": jnp.clip(jnp.exp(jax.random.uniform(key_list[3], (REGIONS, 2), jnp.float32, math.log(0.25), math.log(2.0))), 0.25, 2.0),
    }


time_step = 1.0
feed_rate = 0.04
kill_rate = 0.06


def quad_table(node_total):
    points = [(1.0 - math.cos(math.pi * (target + 1.0) / node_total)) / 2.0 for target in range(node_total)]
    table = []
    for target in range(node_total):
        row_values = []
        for source in range(node_total):
            coeffs = [1.0]
            for other in range(node_total):
                if other != source:
                    divisor = points[source] - points[other]
                    widened = [0.0] * (len(coeffs) + 1)
                    for power in range(len(coeffs)):
                        widened[power + 1] = widened[power + 1] + coeffs[power] / divisor
                        widened[power] = widened[power] - coeffs[power] * points[other] / divisor
                    coeffs = widened
            integral = 0.0
            for power in range(len(coeffs)):
                integral = integral + coeffs[power] * points[target] ** (power + 1) / (power + 1)
            row_values.append(integral)
        table.append(row_values)
    return np.asarray(points, dtype=np.float32), np.asarray(table, dtype=np.float32)


def face_weights(kappa_cells):
    lower_x = (kappa_cells + jnp.roll(kappa_cells, 1, axis=1)) * 0.5
    upper_x = (kappa_cells + jnp.roll(kappa_cells, -1, axis=1)) * 0.5
    lower_z = (kappa_cells + jnp.roll(kappa_cells, 1, axis=2)) * 0.5
    upper_z = (kappa_cells + jnp.roll(kappa_cells, -1, axis=2)) * 0.5
    lower_y = (kappa_cells + jnp.roll(kappa_cells, 1, axis=3)) * 0.5
    upper_y = (kappa_cells + jnp.roll(kappa_cells, -1, axis=3)) * 0.5
    weight_total = lower_x + upper_x + lower_z + upper_z + lower_y + upper_y
    return (lower_x, upper_x, lower_z, upper_z, lower_y, upper_y), weight_total


def full_neighbours(values, weights):
    lower_x, upper_x, lower_z, upper_z, lower_y, upper_y = weights
    summed = lower_x * jnp.roll(values, 1, axis=2) + upper_x * jnp.roll(values, -1, axis=2)
    summed = summed + lower_z * jnp.roll(values, 1, axis=3) + upper_z * jnp.roll(values, -1, axis=3)
    summed = summed + lower_y * jnp.roll(values, 1, axis=4) + upper_y * jnp.roll(values, -1, axis=4)
    return summed


def reaction(values):
    substrate = values[:, 0]
    catalyst = values[:, 1]
    product = substrate * catalyst * catalyst
    grow_sub = -product + feed_rate * (1.0 - substrate)
    grow_cat = product - (feed_rate + kill_rate) * catalyst
    return jnp.stack([grow_sub, grow_cat], axis=1)


def reference(initial, node_guess, region_codes, coeff_table):
    node_total = node_guess.shape[0]
    points, quadrature = quad_table(node_total)
    quadrature = jnp.asarray(quadrature)
    implicit_scale = (time_step * jnp.asarray(points)).reshape(node_total, 1, 1, 1, 1)
    kappa_cells = jnp.moveaxis(coeff_table[region_codes], -1, 0)
    weights, weight_total = face_weights(kappa_cells)
    iterate = node_guess
    for sweep_index in range(SWEEPS):
        summed = full_neighbours(iterate, weights)
        laplace = summed - weight_total * iterate
        derivative = laplace + reaction(iterate)
        integral = jnp.einsum("mj,jfxzy->mfxzy", quadrature, derivative, precision=lax.Precision.HIGHEST)
        rhs_values = initial[None] + time_step * integral - implicit_scale * laplace
        current = iterate
        for inner_index in range(JACOBI):
            summed = full_neighbours(current, weights)
            current = (rhs_values + implicit_scale * summed) / (1.0 + implicit_scale * weight_total)
        iterate = current
    return iterate
```

```python
import functools
import math

import jax
import jax.numpy as jnp
import numpy as np
from jax import lax
from jax.experimental import pallas as pl
from jax.experimental.pallas import tpu as pltpu
from jax.sharding import PartitionSpec as P

SWEEPS = 2
JACOBI = 6

time_step = 1.0
feed_rate = 0.04
kill_rate = 0.06

LANES = 128


def quad_table(node_total):
    points = [
        (1.0 - math.cos(math.pi * (target + 1.0) / node_total)) / 2.0
        for target in range(node_total)
    ]
    table = []
    for target in range(node_total):
        row_values = []
        for source in range(node_total):
            coeffs = [1.0]
            for other in range(node_total):
                if other != source:
                    divisor = points[source] - points[other]
                    widened = [0.0] * (len(coeffs) + 1)
                    for power in range(len(coeffs)):
                        widened[power + 1] = widened[power + 1] + coeffs[power] / divisor
                        widened[power] = widened[power] - coeffs[power] * points[other] / divisor
                    coeffs = widened
            integral = 0.0
            for power in range(len(coeffs)):
                integral = integral + coeffs[power] * points[target] ** (power + 1) / (power + 1)
            row_values.append(integral)
        table.append(row_values)
    return (np.asarray(points, dtype=np.float32), np.asarray(table, dtype=np.float32))


def kernel(
    ring,
    spaces,
    initial_ref,
    guess_ref,
    codes_ref,
    coeff_ref,
    out_ref,
    state,
    rhs,
    gain,
    weight,
    total,
    kappa,
    packed,
    edge,
    in_send,
    in_recv,
    out_send,
    out_recv,
    kap_send,
    kap_recv,
    halo_send,
    halo_recv,
):
    mine = guess_ref.shape[0]
    nodes = mine * ring
    planes, depth = guess_ref.shape[2], guess_ref.shape[3]
    regions = coeff_ref.shape[0]
    points, quad = quad_table(nodes)
    scales = [float(np.float32(time_step) * points[m]) for m in range(nodes)]

    me = lax.axis_index("node")
    here = lax.axis_index("space")
    right = lax.rem(here + 1, spaces)
    left = lax.rem(here + spaces - 1, spaces)
    above = lax.rem(me + 1, ring)
    below = lax.rem(me + ring - 1, ring)

    def block(index):
        return pl.ds(pl.multiple_of(index * LANES, LANES), LANES)

    def remote(src, dst, send, recv, where):
        return pltpu.make_async_remote_copy(
            src_ref=src,
            dst_ref=dst,
            send_sem=send,
            recv_sem=recv,
            device_id=where,
            device_id_type=pl.DeviceIdType.MESH,
        )

    barrier = pltpu.get_barrier_semaphore()
    friends = [(lax.rem(me + step, ring), here) for step in range(1, ring)]
    friends += [(me, left), (me, right)]
    for friend in friends:
        pl.semaphore_signal(
            barrier, inc=1, device_id=friend, device_id_type=pl.DeviceIdType.MESH
        )
    pl.semaphore_wait(barrier, len(friends))

    inward = []
    for step in range(1, ring):
        target = lax.rem(me + step, ring)
        for k in range(mine):
            inward.append(
                remote(
                    guess_ref.at[k, :, :, :, block(target)],
                    state.at[0, :, me * mine + k, pl.ds(1, planes)],
                    in_send.at[step - 1, k],
                    in_recv.at[step - 1, k],
                    (target, here),
                )
            )
    for copy in inward:
        copy.start()

    row = (depth, LANES)
    lane = lax.broadcasted_iota(jnp.int32, row, 1)
    first_lane = lane == 0
    last_lane = lane == LANES - 1
    odd_lane = lax.rem(lane, 2) == 1
    pair = lane // 2
    lane_group = lane // (2 * nodes)

    def lookup(codes, f):
        found = jnp.full(row, coeff_ref[0, f], jnp.float32)
        for r in range(1, regions):
            found = jnp.where(codes == r, coeff_ref[r, f], found)
        return found

    def fill(x, carry):
        center = codes_ref[x, :, block(me)]
        before = codes_ref[x, :, block(below)]
        after = codes_ref[x, :, block(above)]
        low = jnp.where(first_lane, pltpu.roll(before, 1, 1), pltpu.roll(center, 1, 1))
        high = jnp.where(
            last_lane, pltpu.roll(after, LANES - 1, 1), pltpu.roll(center, LANES - 1, 1)
        )
        for f in range(2):
            kappa[f, x + 1] = lookup(center, f)
            weight[4, f, x] = lookup(low, f)
            weight[5, f, x] = lookup(high, f)
            for k in range(mine):
                state[0, f, me * mine + k, x + 1] = guess_ref[k, f, x, :, block(me)]
        return carry

    lax.fori_loop(0, planes, fill, 0)
    kap = [
        remote(
            kappa.at[:, 1], kappa.at[:, planes + 1], kap_send.at[0], kap_recv.at[0], (me, left)
        ),
        remote(kappa.at[:, planes], kappa.at[:, 0], kap_send.at[1], kap_recv.at[1], (me, right)),
    ]
    for copy in kap:
        copy.start()
    for copy in kap:
        copy.wait()

    def build(x, carry):
        for f in range(2):
            center = kappa[f, x + 1]
            faces = [
                (center + kappa[f, x]) * 0.5,
                (center + kappa[f, x + 2]) * 0.5,
                (center + pltpu.roll(center, 1, 0)) * 0.5,
                (center + pltpu.roll(center, depth - 1, 0)) * 0.5,
                (center + weight[4, f, x]) * 0.5,
                (center + weight[5, f, x]) * 0.5,
            ]
            summed = faces[0]
            for face in faces[1:]:
                summed = summed + face
            for side in range(6):
                weight[side, f, x] = faces[side]
            total[f, x] = summed
            for m in range(nodes):
                gain[f, m, x] = scales[m] / (1.0 + scales[m] * summed)
        return carry

    lax.fori_loop(0, planes, build, 0)

    def halo(slot, f):
        return [
            remote(
                state.at[slot, f, :, 1],
                state.at[slot, f, :, planes + 1],
                halo_send.at[slot, f, 0],
                halo_recv.at[slot, f, 0],
                (me, left),
            ),
            remote(
                state.at[slot, f, :, planes],
                state.at[slot, f, :, 0],
                halo_send.at[slot, f, 1],
                halo_recv.at[slot, f, 1],
                (me, right),
            ),
            remote(
                packed.at[slot, f],
                edge.at[slot, f, 0],
                halo_send.at[slot, f, 2],
                halo_recv.at[slot, f, 2],
                (above, here),
            ),
            remote(
                packed.at[slot, f],
                edge.at[slot, f, 1],
                halo_send.at[slot, f, 3],
                halo_recv.at[slot, f, 3],
                (below, here),
            ),
        ]

    def pack(values, slot, f, x):
        gathered = pltpu.roll(values[0], 1, 1)
        for m in range(1, nodes):
            gathered = jnp.where(pair == m, pltpu.roll(values[m], 2 * m + 1, 1), gathered)
        spread = pltpu.roll(gathered, x * (2 * nodes), 1)
        packed[slot, f] = jnp.where(lane_group == x, spread, packed[slot, f])

    def edges(slot, f):
        low = pltpu.roll(edge[slot, f, 0], 1, 1)
        high = pltpu.roll(edge[slot, f, 1], LANES - 1, 1)
        return jnp.where(odd_lane, low, high)

    def edges_at(both, x):
        return pltpu.roll(both, lax.rem((planes - x) * (2 * nodes), LANES), 1)

    def neighbours(slot, f, m, x, faces, ends):
        center = state[slot, f, m, x + 1]
        tips = pltpu.roll(ends, LANES - (2 * m + 1), 1)
        low = jnp.where(first_lane, tips, pltpu.roll(center, 1, 1))
        high = jnp.where(last_lane, tips, pltpu.roll(center, LANES - 1, 1))
        summed = faces[0] * state[slot, f, m, x] + faces[1] * state[slot, f, m, x + 2]
        summed = summed + (
            faces[2] * pltpu.roll(center, 1, 0) + faces[3] * pltpu.roll(center, depth - 1, 0)
        )
        return center, summed + (faces[4] * low + faces[5] * high)

    def opening(slot, f):
        both = edges(slot, f)

        def step(x, carry):
            faces = [weight[side, f, x] for side in range(6)]
            ends = edges_at(both, x)
            weight_total = total[f, x]
            laplaces, slopes = [], []
            for m in range(nodes):
                center, summed = neighbours(slot, f, m, x, faces, ends)
                laplace = summed - weight_total * center
                substrate = state[slot, 0, m, x + 1]
                catalyst = state[slot, 1, m, x + 1]
                product = substrate * catalyst * catalyst
                if f == 0:
                    grow = -product + feed_rate * (1.0 - substrate)
                else:
                    grow = product - (feed_rate + kill_rate) * catalyst
                laplaces.append(laplace)
                slopes.append(laplace + grow)
            start = initial_ref[f, x, :, block(me)]
            fresh = []
            for m in range(nodes):
                base = float(quad[m, 0]) * slopes[0]
                for j in range(1, nodes):
                    base = base + float(quad[m, j]) * slopes[j]
                base = start + time_step * base
                inverse = 1.0 / (1.0 + scales[m] * weight_total)
                rhs[f, m, x] = (base - scales[m] * laplaces[m]) * inverse
                center = state[slot, f, m, x + 1]
                value = (base + scales[m] * (weight_total * center)) * inverse
                state[1 - slot, f, m, x + 1] = value
                fresh.append(value)
            pack(fresh, 1 - slot, f, x)
            return carry

        lax.fori_loop(0, planes, step, 0)

    def relax(slot, f):
        both = edges(slot, f)

        def step(x, carry):
            faces = [weight[side, f, x] for side in range(6)]
            ends = edges_at(both, x)
            fresh = []
            for m in range(nodes):
                _, summed = neighbours(slot, f, m, x, faces, ends)
                value = rhs[f, m, x] + gain[f, m, x] * summed
                state[1 - slot, f, m, x + 1] = value
                fresh.append(value)
            pack(fresh, 1 - slot, f, x)
            return carry

        lax.fori_loop(0, planes, step, 0)

    def outward(f):
        copies = []
        for step in range(1, ring):
            target = lax.rem(me + step, ring)
            copies.append(
                remote(
                    state.at[0, f, pl.ds(target * mine, mine), pl.ds(1, planes)],
                    out_ref.at[:, f, :, :, block(me)],
                    out_send.at[step - 1, f],
                    out_recv.at[step - 1, f],
                    (target, here),
                )
            )
        return copies

    packed[...] = jnp.zeros(packed.shape, jnp.float32)
    for copy in inward:
        copy.wait_recv()

    for f in range(2):

        def first_pack(x, carry, f=f):
            pack([state[0, f, m, x + 1] for m in range(nodes)], 0, f, x)
            return carry

        lax.fori_loop(0, planes, first_pack, 0)
        for copy in halo(0, f):
            copy.start()

    last_step = SWEEPS * JACOBI - 1
    for sweep in range(SWEEPS):
        slot = (sweep * JACOBI) % 2
        for f in range(2):
            for copy in halo(slot, f):
                copy.wait_recv()
            if sweep > 0:
                for copy in halo(1 - slot, f):
                    copy.wait_send()
            opening(slot, f)
            for copy in halo(1 - slot, f):
                copy.start()

        def inner(t, carry, sweep=sweep):
            e = sweep * JACOBI + 1 + t // 2
            f = lax.rem(t, 2)
            slot = lax.rem(e, 2)
            for copy in halo(slot, f):
                copy.wait_recv()
            for copy in halo(1 - slot, f):
                copy.wait_send()
            relax(slot, f)
            for copy in halo(1 - slot, f):
                copy.start()
            return carry

        rounds = JACOBI - 1 if sweep < SWEEPS - 1 else JACOBI - 2
        lax.fori_loop(0, 2 * rounds, inner, 0)

    slot = last_step % 2
    for f in range(2):
        for copy in halo(slot, f):
            copy.wait_recv()
        for copy in halo(1 - slot, f):
            copy.wait_send()
        relax(slot, f)
        for copy in outward(f):
            copy.start()

        def keep(x, carry, f=f):
            for k in range(mine):
                out_ref[k, f, x, :, block(me)] = state[0, f, me * mine + k, x + 1]
            return carry

        lax.fori_loop(0, planes, keep, 0)

    for copy in inward:
        copy.wait_send()
    for f in range(2):
        for copy in halo(slot, f):
            copy.wait_send()
        for copy in outward(f):
            copy.wait()


def body(ring, spaces, initial, node_guess, region_codes, coeff_table):
    mine, fields, planes, depth, width = node_guess.shape
    nodes = mine * ring
    vmem = pltpu.VMEM
    f32 = jnp.float32
    dma = pltpu.SemaphoreType.DMA
    in_vmem = pl.BlockSpec(memory_space=pltpu.VMEM)
    return pl.pallas_call(
        functools.partial(kernel, ring, spaces),
        out_shape=jax.ShapeDtypeStruct(node_guess.shape, f32),
        in_specs=[in_vmem, in_vmem, in_vmem, pl.BlockSpec(memory_space=pltpu.SMEM)],
        out_specs=in_vmem,
        scratch_shapes=[
            vmem((2, fields, nodes, planes + 2, depth, LANES), f32),
            vmem((fields, nodes, planes, depth, LANES), f32),
            vmem((fields, nodes, planes, depth, LANES), f32),
            vmem((6, fields, planes, depth, LANES), f32),
            vmem((fields, planes, depth, LANES), f32),
            vmem((fields, planes + 2, depth, LANES), f32),
            vmem((2, fields, depth, LANES), f32),
            vmem((2, fields, 2, depth, LANES), f32),
            dma((ring - 1, mine)),
            dma((ring - 1, mine)),
            dma((ring - 1, fields)),
            dma((ring - 1, fields)),
            dma((2,)),
            dma((2,)),
            dma((2, fields, 4)),
            dma((2, fields, 4)),
        ],
        compiler_params=pltpu.CompilerParams(
            collective_id=0, has_side_effects=True, vmem_limit_bytes=32 * 1024 * 1024
        ),
    )(initial, node_guess, region_codes, coeff_table)


def solution(mesh):
    in_specs = (
        P(None, "space", None, None),
        P("node", None, "space", None, None),
        P("space", None, None),
        P(),
    )
    out_specs = P("node", None, "space", None, None)
    run = functools.partial(body, mesh.shape["node"], mesh.shape["space"])
    return jax.shard_map(run, mesh=mesh, in_specs=in_specs, out_specs=out_specs, check_vma=False)
```

```python
import functools
import math

import jax
import jax.numpy as jnp
import numpy as np
from jax import lax
from jax.experimental import pallas as pl
from jax.experimental.pallas import tpu as pltpu
from jax.sharding import PartitionSpec as P

SWEEPS = 2
JACOBI = 6

time_step = 1.0
feed_rate = 0.04
kill_rate = 0.06

LANES = 128


def quad_table(node_total):
    points = [
        (1.0 - math.cos(math.pi * (target + 1.0) / node_total)) / 2.0
        for target in range(node_total)
    ]
    table = []
    for target in range(node_total):
        row_values = []
        for source in range(node_total):
            coeffs = [1.0]
            for other in range(node_total):
                if other != source:
                    divisor = points[source] - points[other]
                    widened = [0.0] * (len(coeffs) + 1)
                    for power in range(len(coeffs)):
                        widened[power + 1] = widened[power + 1] + coeffs[power] / divisor
                        widened[power] = widened[power] - coeffs[power] * points[other] / divisor
                    coeffs = widened
            integral = 0.0
            for power in range(len(coeffs)):
                integral = integral + coeffs[power] * points[target] ** (power + 1) / (power + 1)
            row_values.append(integral)
        table.append(row_values)
    return (np.asarray(points, dtype=np.float32), np.asarray(table, dtype=np.float32))


def kernel(
    ring,
    spaces,
    initial_ref,
    guess_ref,
    codes_ref,
    coeff_ref,
    out_ref,
    state_even,
    state_odd,
    rhs,
    gain,
    weight,
    total,
    kappa,
    packed,
    edge,
    in_send,
    in_recv,
    out_send,
    out_recv,
    kap_send,
    kap_recv,
    halo_send,
    halo_recv,
):
    mine = guess_ref.shape[0]
    nodes = mine * ring
    planes, depth = guess_ref.shape[2], guess_ref.shape[3]
    regions = coeff_ref.shape[0]
    points, quad = quad_table(nodes)
    states = (state_even, state_odd)
    scales = [float(np.float32(time_step) * points[m]) for m in range(nodes)]

    me = lax.axis_index("node")
    here = lax.axis_index("space")
    right = lax.rem(here + 1, spaces)
    left = lax.rem(here + spaces - 1, spaces)

    def fold(index):
        return index + (index // 2) * (5 - 2 * index) if ring == 4 else index

    own = fold(me)
    next_block = lax.rem(own + 1, ring)
    last_block = lax.rem(own + ring - 1, ring)
    above = fold(next_block)
    below = fold(last_block)

    def block(index):
        return pl.ds(pl.multiple_of(index * LANES, LANES), LANES)

    def remote(src, dst, send, recv, where):
        return pltpu.make_async_remote_copy(
            src_ref=src,
            dst_ref=dst,
            send_sem=send,
            recv_sem=recv,
            device_id=where,
            device_id_type=pl.DeviceIdType.MESH,
        )

    barrier = pltpu.get_barrier_semaphore()
    friends = [(lax.rem(me + step, ring), here) for step in range(1, ring)]
    friends += [(me, left), (me, right)]
    for friend in friends:
        pl.semaphore_signal(
            barrier, inc=1, device_id=friend, device_id_type=pl.DeviceIdType.MESH
        )
    pl.semaphore_wait(barrier, len(friends))

    inward = []
    for step in range(1, ring):
        target = lax.rem(me + step, ring)
        for k in range(mine):
            inward.append(
                remote(
                    guess_ref.at[k, :, :, :, block(fold(target))],
                    state_even.at[:, me * mine + k, pl.ds(1, planes)],
                    in_send.at[step - 1, k],
                    in_recv.at[step - 1, k],
                    (target, here),
                )
            )
    for copy in inward:
        copy.start()

    row = (depth, LANES)
    lane = lax.broadcasted_iota(jnp.int32, row, 1)
    first_lane = lane == 0
    last_lane = lane == LANES - 1
    odd_lane = lax.rem(lane, 2) == 1
    pair = lane // 2
    lane_group = lane // (2 * nodes)

    def lookup(codes, f):
        found = jnp.full(row, coeff_ref[0, f], jnp.float32)
        for r in range(1, regions):
            found = jnp.where(codes == r, coeff_ref[r, f], found)
        return found

    def fill(x, carry):
        center = codes_ref[x, :, block(own)]
        before = codes_ref[x, :, block(last_block)]
        after = codes_ref[x, :, block(next_block)]
        low = jnp.where(first_lane, pltpu.roll(before, 1, 1), pltpu.roll(center, 1, 1))
        high = jnp.where(
            last_lane, pltpu.roll(after, LANES - 1, 1), pltpu.roll(center, LANES - 1, 1)
        )
        for f in range(2):
            kappa[f, x + 1] = lookup(center, f)
            weight[4, f, x] = lookup(low, f)
            weight[5, f, x] = lookup(high, f)
            for k in range(mine):
                state_even[f, me * mine + k, x + 1] = guess_ref[k, f, x, :, block(own)]
        return carry

    lax.fori_loop(0, planes, fill, 0)
    kap = [
        remote(
            kappa.at[:, 1], kappa.at[:, planes + 1], kap_send.at[0], kap_recv.at[0], (me, left)
        ),
        remote(kappa.at[:, planes], kappa.at[:, 0], kap_send.at[1], kap_recv.at[1], (me, right)),
    ]
    for copy in kap:
        copy.start()
    for copy in kap:
        copy.wait()

    def build(x, carry):
        for f in range(2):
            center = kappa[f, x + 1]
            faces = [
                (center + kappa[f, x]) * 0.5,
                (center + kappa[f, x + 2]) * 0.5,
                (center + pltpu.roll(center, 1, 0)) * 0.5,
                (center + pltpu.roll(center, depth - 1, 0)) * 0.5,
                (center + weight[4, f, x]) * 0.5,
                (center + weight[5, f, x]) * 0.5,
            ]
            summed = faces[0]
            for face in faces[1:]:
                summed = summed + face
            for side in range(6):
                weight[side, f, x] = faces[side]
            total[f, x] = summed
            for m in range(nodes):
                gain[f, m, x] = scales[m] / (1.0 + scales[m] * summed)
        return carry

    lax.fori_loop(0, planes, build, 0)

    def halo(slot, f):
        return [
            remote(
                states[slot].at[f, :, 1],
                states[slot].at[f, :, planes + 1],
                halo_send.at[slot, f, 0],
                halo_recv.at[slot, f, 0],
                (me, left),
            ),
            remote(
                states[slot].at[f, :, planes],
                states[slot].at[f, :, 0],
                halo_send.at[slot, f, 1],
                halo_recv.at[slot, f, 1],
                (me, right),
            ),
            remote(
                packed.at[slot, f],
                edge.at[slot, f, 0],
                halo_send.at[slot, f, 2],
                halo_recv.at[slot, f, 2],
                (above, here),
            ),
            remote(
                packed.at[slot, f],
                edge.at[slot, f, 1],
                halo_send.at[slot, f, 3],
                halo_recv.at[slot, f, 3],
                (below, here),
            ),
        ]

    def gather(values):
        gathered = pltpu.roll(values[0], 1, 1)
        for m in range(1, nodes):
            gathered = jnp.where(pair == m, pltpu.roll(values[m], 2 * m + 1, 1), gathered)
        return gathered

    def pack(rows, slot, f):
        whole = rows[0]
        for x in range(1, planes):
            spread = pltpu.roll(rows[x], x * (2 * nodes), 1)
            whole = jnp.where(lane_group == x, spread, whole)
        packed[slot, f] = whole

    def edges(slot, f):
        low = pltpu.roll(edge[slot, f, 0], 1, 1)
        high = pltpu.roll(edge[slot, f, 1], LANES - 1, 1)
        return jnp.where(odd_lane, low, high)

    def edges_at(both, x):
        shift = ((planes - x) * (2 * nodes)) % LANES
        return pltpu.roll(both, shift, 1) if shift else both

    def neighbours(slot, f, m, x, faces, ends):
        center = states[slot][f, m, x + 1]
        tips = pltpu.roll(ends, LANES - (2 * m + 1), 1)
        low = jnp.where(first_lane, tips, pltpu.roll(center, 1, 1))
        high = jnp.where(last_lane, tips, pltpu.roll(center, LANES - 1, 1))
        summed = faces[0] * states[slot][f, m, x] + faces[1] * states[slot][f, m, x + 2]
        summed = summed + (
            faces[2] * pltpu.roll(center, 1, 0) + faces[3] * pltpu.roll(center, depth - 1, 0)
        )
        return center, summed + (faces[4] * low + faces[5] * high)

    def opening(slot, f):
        both = edges(slot, f)
        rows = []
        for x in range(planes):
            faces = [weight[side, f, x] for side in range(6)]
            ends = edges_at(both, x)
            weight_total = total[f, x]
            laplaces, slopes = [], []
            for m in range(nodes):
                center, summed = neighbours(slot, f, m, x, faces, ends)
                laplace = summed - weight_total * center
                substrate = states[slot][0, m, x + 1]
                catalyst = states[slot][1, m, x + 1]
                product = substrate * catalyst * catalyst
                if f == 0:
                    grow = -product + feed_rate * (1.0 - substrate)
                else:
                    grow = product - (feed_rate + kill_rate) * catalyst
                laplaces.append(laplace)
                slopes.append(laplace + grow)
            start = initial_ref[f, x, :, block(own)]
            fresh = []
            for m in range(nodes):
                base = float(quad[m, 0]) * slopes[0]
                for j in range(1, nodes):
                    base = base + float(quad[m, j]) * slopes[j]
                base = start + time_step * base
                inverse = 1.0 / (1.0 + scales[m] * weight_total)
                rhs[f, m, x] = (base - scales[m] * laplaces[m]) * inverse
                center = states[slot][f, m, x + 1]
                value = (base + scales[m] * (weight_total * center)) * inverse
                states[1 - slot][f, m, x + 1] = value
                fresh.append(value)
            rows.append(gather(fresh))
        pack(rows, 1 - slot, f)

    def relax(slot, f):
        both = edges(slot, f)
        rows = []
        for x in range(planes):
            faces = [weight[side, f, x] for side in range(6)]
            ends = edges_at(both, x)
            fresh = []
            for m in range(nodes):
                _, summed = neighbours(slot, f, m, x, faces, ends)
                value = rhs[f, m, x] + gain[f, m, x] * summed
                states[1 - slot][f, m, x + 1] = value
                fresh.append(value)
            rows.append(gather(fresh))
        pack(rows, 1 - slot, f)

    def outward(f):
        copies = []
        for step in range(1, ring):
            target = lax.rem(me + step, ring)
            copies.append(
                remote(
                    state_even.at[f, pl.ds(target * mine, mine), pl.ds(1, planes)],
                    out_ref.at[:, f, :, :, block(own)],
                    out_send.at[step - 1, f],
                    out_recv.at[step - 1, f],
                    (target, here),
                )
            )
        return copies

    for copy in inward:
        copy.wait_recv()

    for f in range(2):
        pack(
            [gather([state_even[f, m, x + 1] for m in range(nodes)]) for x in range(planes)], 0, f
        )
        for copy in halo(0, f):
            copy.start()

    def advance(slot, f):
        for copy in halo(slot, f):
            copy.wait_recv()
        for copy in halo(1 - slot, f):
            copy.wait_send()
        relax(slot, f)

    def send(slot, f):
        for copy in halo(slot, f):
            copy.start()

    def both_fields(slot):
        def one(f, carry):
            advance(slot, f)
            send(1 - slot, f)
            return carry

        lax.fori_loop(0, 2, one, 0)

    for sweep in range(SWEEPS):
        for f in range(2):
            for copy in halo(0, f):
                copy.wait_recv()
            if sweep > 0:
                for copy in halo(1, f):
                    copy.wait_send()
            opening(0, f)
            send(1, f)

        def inner(t, carry):
            both_fields(1)
            both_fields(0)
            return carry

        lax.fori_loop(0, (JACOBI - 2) // 2, inner, 0)
        if sweep < SWEEPS - 1:
            both_fields(1)

    slot = 1
    for f in range(2):
        advance(slot, f)
        for copy in outward(f):
            copy.start()

        def keep(x, carry, f=f):
            for k in range(mine):
                out_ref[k, f, x, :, block(own)] = state_even[f, me * mine + k, x + 1]
            return carry

        lax.fori_loop(0, planes, keep, 0)

    for copy in inward:
        copy.wait_send()
    for f in range(2):
        for copy in halo(slot, f):
            copy.wait_send()
        for copy in outward(f):
            copy.wait()


def body(ring, spaces, initial, node_guess, region_codes, coeff_table):
    mine, fields, planes, depth, width = node_guess.shape
    nodes = mine * ring
    vmem = pltpu.VMEM
    f32 = jnp.float32
    dma = pltpu.SemaphoreType.DMA
    in_vmem = pl.BlockSpec(memory_space=pltpu.VMEM)
    return pl.pallas_call(
        functools.partial(kernel, ring, spaces),
        out_shape=jax.ShapeDtypeStruct(node_guess.shape, f32),
        in_specs=[in_vmem, in_vmem, in_vmem, pl.BlockSpec(memory_space=pltpu.SMEM)],
        out_specs=in_vmem,
        scratch_shapes=[
            vmem((fields, nodes, planes + 2, depth, LANES), f32),
            vmem((fields, nodes, planes + 2, depth, LANES), f32),
            vmem((fields, nodes, planes, depth, LANES), f32),
            vmem((fields, nodes, planes, depth, LANES), f32),
            vmem((6, fields, planes, depth, LANES), f32),
            vmem((fields, planes, depth, LANES), f32),
            vmem((fields, planes + 2, depth, LANES), f32),
            vmem((2, fields, depth, LANES), f32),
            vmem((2, fields, 2, depth, LANES), f32),
            dma((ring - 1, mine)),
            dma((ring - 1, mine)),
            dma((ring - 1, fields)),
            dma((ring - 1, fields)),
            dma((2,)),
            dma((2,)),
            dma((2, fields, 4)),
            dma((2, fields, 4)),
        ],
        compiler_params=pltpu.CompilerParams(
            collective_id=0, has_side_effects=True, vmem_limit_bytes=32 * 1024 * 1024
        ),
    )(initial, node_guess, region_codes, coeff_table)


def solution(mesh):
    in_specs = (
        P(None, "space", None, None),
        P("node", None, "space", None, None),
        P("space", None, None),
        P(),
    )
    out_specs = P("node", None, "space", None, None)
    run = functools.partial(body, mesh.shape["node"], mesh.shape["space"])
    return jax.shard_map(run, mesh=mesh, in_specs=in_specs, out_specs=out_specs, check_vma=False)
```
